512 devices in a mesh: dom: 64 (over x, y, core), ch: 8 (over z).
Axes of the slice: x: 4, y: 8, z: 8, core: 2. Of those that a mesh axis runs over, the one named last changes fastest.
Arguments:
- features: bfloat16 [25, 128, 98304], P(None, 'ch', 'dom'), may hold values from -6 to 6
- neighbours: int32 [32, 32768], P(None, 'dom'), may hold values from 0 to 98303, as said below
- pad_mask: int32 [32, 32768], P(None, 'dom'), may hold values 0 or 1
- displacement: float32 [3, 32, 32768], P(None, None, 'dom'), may hold values from -1.5 to 1.5
- radial_weight: float32 [8, 5, 128], P(None, None, 'ch'), may hold values from -2 to 2
- mixing_weight: bfloat16 [128, 128], replicated, may hold values from -0.5 to 0.5
- readout_weight: float32 [128], P('ch'), may hold values from -0.5 to 0.5
Outputs:
- density: float32 [32768], P('dom')
The draws below stay inside these ranges and needn't reach their ends.
Inputs may be any that keep to these rules, and one draw needn't show every extreme that they name: `neighbours`: atom a lies in domain a // 1536 and probe p in brick p // 512; every neighbour of a probe lies in the domain of the probe's brick or in one of the two domains on either side of it, counted cyclically over the 64 domains.
All inputs are finite; a program needn't handle non-finite values. No bound on the sum of `pad_mask` on one device may be relied on, other than what follows from the above.
Results may differ from the reference program's by a relative error of at most 0.0003.
Values may be sent and summed in bfloat16 or wider, within the bound.
A program may use at most 64 MiB of HBM per device.

```python
import jax
import jax.numpy as jnp
from jax import lax

CH = 128
COMPS = 25
NB = 8
K = 32
ATOM_DEV = 1536
PROBE_DEV = 512
ATOMS = 98304
PROBES = 32768


def draw_neighbours(key, part):
    key = jax.random.fold_in(key, 11)
    key_offset, key_atom = jax.random.split(key)
    offset = jax.random.randint(key_offset, (K, PROBES), -2, 3)
    local_atom = jax.random.randint(key_atom, (K, PROBES), 0, ATOM_DEV)
    count_dom = PROBES // PROBE_DEV
    domain = (jnp.arange(PROBES, dtype=jnp.int32) // PROBE_DEV)[None, :]
    atom_ids = (domain + offset) % count_dom * ATOM_DEV + local_atom
    atom_ids = atom_ids.at[0, 0].set(0)
    atom_ids = atom_ids.at[K - 1, PROBES - 1].set(count_dom * ATOM_DEV - 1)
    return atom_ids.astype(jnp.int32)


def set_ends(entries, key, smallest, high):
    shape = entries.shape
    place = [jax.random.randint(jax.random.fold_in(key, axis), (), 0, shape[axis]) for axis in range(len(shape))]
    entries = entries.at[tuple(place)].set(smallest)
    longest = shape.index(max(shape))
    place[longest] = (place[longest] + 1) % shape[longest]
    return entries.at[tuple(place)].set(high)


def block_scale(stream_key, shape, cuts, smallest, largest):
    factor_of, own = 1.0, jax.random.fold_in(stream_key, 6)
    for dim, shards_of in cuts:
        steps = jnp.exp(jax.random.uniform(jax.random.fold_in(own, dim), (shards_of,), jnp.float32, smallest / len(cuts), largest / len(cuts)))
        factor_of = factor_of * jnp.repeat(steps, shape[dim] // shards_of).reshape([-1 if axis == dim else 1 for axis in range(len(shape))])
    return factor_of


def noise(key, shape, width, most, shards=(), kind=jnp.bfloat16):
    values = width * jax.random.normal(key, shape, jnp.float32)
    if shards:
        values = values * block_scale(key, shape, shards, -0.22, 0.18)
    return jnp.clip(values, -most, most).astype(kind)


def setup_inputs(seed: int = 0) -> dict:
    splits = jax.random.split(jax.random.key(seed), 8)
    return {
        "features": noise(splits[0], (COMPS, CH, ATOMS), 1.0, 6.0, ((1, 8), (2, 64))),
        "neighbours": draw_neighbours(jax.random.fold_in(splits[7], 71), 0),
        "pad_mask": set_ends((jax.random.randint(splits[2], (K, PROBES), 0, 4) < 3).astype(jnp.int32), jax.random.fold_in(splits[2], 1), 0, 1),
        "displacement": jnp.clip(jax.random.uniform(splits[3], (3, K, PROBES), jnp.float32, -1.5, 1.5) * block_scale(splits[3], (3, K, PROBES), ((2, 64),), -0.4, 0.0), -1.5, 1.5),
        "radial_weight": noise(splits[4], (NB, 5, CH), NB ** -0.5, 2.0, ((2, 8),), jnp.float32),
        "mixing_weight": noise(splits[5], (CH, CH), CH ** -0.5, 0.5),
        "readout_weight": noise(splits[6], (CH,), CH ** -0.5, 0.5, ((0, 8),), jnp.float32),
    }


degree_bounds = ((0, 1), (1, 4), (4, 9), (9, 16), (16, 25))


def harmonics(coords):
    coord_x, coord_y, coord_z = coords[0], coords[1], coords[2]
    square_x = coord_x * coord_x
    square_y = coord_y * coord_y
    square_z = coord_z * coord_z
    radius_sq = square_x + square_y + square_z
    components = [
        jnp.ones_like(coord_x),
        coord_x, coord_y, coord_z,
        coord_x * coord_y, coord_y * coord_z, (3.0 * square_z - radius_sq) * 0.2887,
        coord_x * coord_z, 0.5 * (square_x - square_y),
        coord_y * (3.0 * square_x - square_y) * 0.2, coord_x * coord_y * coord_z,
        coord_y * (4.0 * square_z - square_x - square_y) * 0.15,
        coord_z * (2.0 * square_z - 3.0 * square_x - 3.0 * square_y) * 0.15,
        coord_x * (4.0 * square_z - square_x - square_y) * 0.15,
        0.5 * coord_z * (square_x - square_y), coord_x * (square_x - 3.0 * square_y) * 0.2,
        coord_x * coord_y * (square_x - square_y) * 0.5,
        coord_y * coord_z * (3.0 * square_x - square_y) * 0.2,
        coord_x * coord_y * (7.0 * square_z - radius_sq) * 0.1,
        coord_y * coord_z * (7.0 * square_z - 3.0 * radius_sq) * 0.1,
        (35.0 * square_z * square_z - 30.0 * square_z * radius_sq + 3.0 * radius_sq * radius_sq) * 0.02,
        coord_x * coord_z * (7.0 * square_z - 3.0 * radius_sq) * 0.1,
        (square_x - square_y) * (7.0 * square_z - radius_sq) * 0.05,
        coord_x * coord_z * (square_x - 3.0 * square_y) * 0.2,
        (square_x * square_x - 6.0 * square_x * square_y + square_y * square_y) * 0.1,
    ]
    return jnp.stack(components)


def gaussians_of(coords, count_basis):
    radius_sq = coords[0] * coords[0] + coords[1] * coords[1] + coords[2] * coords[2]
    centers = 0.9 * jnp.arange(count_basis, dtype=jnp.float32)
    spread = radius_sq[None] - centers.reshape((count_basis,) + (1,) * radius_sq.ndim)
    return jnp.exp(-(spread * spread))


def probe_block(features, neighbour_block, mask_block, disp_block, radial_weight):
    harmonic = harmonics(disp_block)
    gaussian = gaussians_of(disp_block, radial_weight.shape[0])
    gathered = features[:, :, neighbour_block].astype(jnp.float32)
    summed = jnp.zeros(gathered.shape[1:], jnp.float32)
    for degree in range(5):
        first_comp, last_comp = degree_bounds[degree]
        projection = jnp.sum(gathered[first_comp:last_comp] * harmonic[first_comp:last_comp, None], axis=0)
        radial_part = jnp.einsum("jc,jkb->ckb", radial_weight[:, degree, :], gaussian)
        summed = summed + radial_part * projection
    summed = summed * mask_block.astype(jnp.float32)[None]
    return jnp.sum(summed, axis=1) * (1.0 / K)


def reference(features, neighbours, pad_mask, displacement, radial_weight, mixing_weight, readout_weight):
    count_blocks = PROBES // PROBE_DEV
    neighbour_blocks = jnp.moveaxis(neighbours.reshape(K, count_blocks, PROBE_DEV), 1, 0)
    mask_blocks = jnp.moveaxis(pad_mask.reshape(K, count_blocks, PROBE_DEV), 1, 0)
    disp_blocks = jnp.moveaxis(displacement.reshape(3, K, count_blocks, PROBE_DEV), 2, 0)

    def one_block(inputs):
        return probe_block(features, inputs[0], inputs[1], inputs[2], radial_weight)

    results = lax.map(one_block, (neighbour_blocks, mask_blocks, disp_blocks))
    probe_field = jnp.moveaxis(results, 0, 1).reshape(CH, PROBES)
    mixed = jnp.dot(mixing_weight.astype(jnp.float32).T, probe_field, precision=lax.Precision.HIGHEST)
    return jnp.sum(readout_weight[:, None] * jax.nn.silu(mixed), axis=0)
```

```python
import functools

import jax
import jax.numpy as jnp
from jax import lax
from jax.experimental import pallas as pl
from jax.experimental.pallas import tpu as pltpu
from jax.sharding import PartitionSpec as P

COMPS = 25
CHAN = 16
ROWS = COMPS * CHAN
ATOMS = 1536
PROBES = 512
SLOTS = 32
BASIS = 8
WINDOWS = 5
CHUNK = 256
CHUNKS = ATOMS // CHUNK
HALF = CHUNKS // 2
PAD = 4
TABLE_ROWS = PAD + WINDOWS * ATOMS * 4 + PAD
SLOT_ROWS = PROBES * 4
PEERS = 8
UNROLL = 4
DEGREES = ((0, 1), (1, 4), (4, 9), (9, 16), (16, 25))
MESH = pl.DeviceIdType.MESH
f32 = jnp.float32
bf16 = jnp.bfloat16


def harmonics(coord_x, coord_y, coord_z):
    square_x = coord_x * coord_x
    square_y = coord_y * coord_y
    square_z = coord_z * coord_z
    radius_sq = square_x + square_y + square_z
    components = [
        jnp.ones_like(coord_x),
        coord_x,
        coord_y,
        coord_z,
        coord_x * coord_y,
        coord_y * coord_z,
        (3.0 * square_z - radius_sq) * 0.2887,
        coord_x * coord_z,
        0.5 * (square_x - square_y),
        coord_y * (3.0 * square_x - square_y) * 0.2,
        coord_x * coord_y * coord_z,
        coord_y * (4.0 * square_z - square_x - square_y) * 0.15,
        coord_z * (2.0 * square_z - 3.0 * square_x - 3.0 * square_y) * 0.15,
        coord_x * (4.0 * square_z - square_x - square_y) * 0.15,
        0.5 * coord_z * (square_x - square_y),
        coord_x * (square_x - 3.0 * square_y) * 0.2,
        coord_x * coord_y * (square_x - square_y) * 0.5,
        coord_y * coord_z * (3.0 * square_x - square_y) * 0.2,
        coord_x * coord_y * (7.0 * square_z - radius_sq) * 0.1,
        coord_y * coord_z * (7.0 * square_z - 3.0 * radius_sq) * 0.1,
        (35.0 * square_z * square_z - 30.0 * square_z * radius_sq + 3.0 * radius_sq * radius_sq)
        * 0.02,
        coord_x * coord_z * (7.0 * square_z - 3.0 * radius_sq) * 0.1,
        (square_x - square_y) * (7.0 * square_z - radius_sq) * 0.05,
        coord_x * coord_z * (square_x - 3.0 * square_y) * 0.2,
        (square_x * square_x - 6.0 * square_x * square_y + square_y * square_y) * 0.1,
    ]
    return components, radius_sq


def iota(shape, dim):
    return lax.broadcasted_iota(jnp.int32, shape, dim)


def split3(value):
    first = value.astype(bf16)
    rest = value - first.astype(f32)
    second = rest.astype(bf16)
    third = (rest - second.astype(f32)).astype(bf16)
    return first, second, third


def dot(left, right, left_dim, right_dim):
    return lax.dot_general(
        left, right, (((left_dim,), (right_dim,)), ((), ())), preferred_element_type=f32
    )


def kernel(
    feat,
    nbr_hbm,
    mask_hbm,
    disp_hbm,
    radial_hbm,
    mixing_hbm,
    readout_hbm,
    out,
    nbr,
    mask,
    disp,
    radial,
    mixing,
    readout,
    win,
    table,
    weights,
    acc,
    feats,
    expand,
    idx_vmem,
    field_all,
    send_read,
    recv_read,
    input_sem,
    win_send,
    win_recv,
    fwd_send,
    own_sem,
    idx_sem,
    peer_send,
    peer_recv,
    *idx,
):
    me = lax.axis_index("dom")
    my_ch = lax.axis_index("ch")
    count = lax.axis_size("dom")
    odd = lax.rem(me, 2)

    def at(offset):
        return lax.rem(me + offset + count, count)

    barrier = pltpu.get_barrier_semaphore()
    for offset in (-2, -1, 1, 2):
        pl.semaphore_signal(barrier, inc=1, device_id={"dom": at(offset)}, device_id_type=MESH)
    for step in range(1, PEERS):
        peer = lax.rem(my_ch + step, PEERS)
        pl.semaphore_signal(barrier, inc=1, device_id={"ch": peer}, device_id_type=MESH)

    input_copies = [
        pltpu.make_async_copy(source, landing, input_sem.at[place])
        for place, (source, landing) in enumerate(
            (
                (nbr_hbm, nbr),
                (mask_hbm, mask),
                (disp_hbm, disp),
                (radial_hbm, radial),
                (mixing_hbm, mixing),
                (readout_hbm, readout),
            )
        )
    ]
    for copy in input_copies:
        copy.start()
    own_copy = pltpu.make_async_copy(feat, win.at[2], own_sem)
    own_copy.start()
    pl.semaphore_wait(barrier, 4 + PEERS - 1)

    def columns(chunk):
        return pl.ds(pl.multiple_of(chunk * CHUNK, CHUNK), CHUNK)

    def send(chunk, slot, target, sems):
        copy = pltpu.make_async_remote_copy(
            src_ref=feat.at[:, columns(chunk)],
            dst_ref=win.at[slot, :, columns(chunk)],
            send_sem=sems,
            recv_sem=win_recv.at[slot, chunk],
            device_id={"dom": target},
            device_id_type=MESH,
        )
        copy.start()
        return copy

    even_case = 1 - odd
    first_target = jnp.where(odd == 1, at(1), at(-2))
    first_slot = jnp.where(odd == 1, 1, 4)
    second_target = jnp.where(odd == 1, at(2), at(-1))
    second_slot = jnp.where(odd == 1, 0, 3)
    whole_target = jnp.where(odd == 1, at(-2), at(2))
    whole_slot = jnp.where(odd == 1, 4, 0)
    sibling = jnp.where(odd == 1, at(-1), at(1))
    sibling_slot = jnp.where(odd == 1, 3, 1)

    copies = []
    for step in range(HALF):
        copies.append(send(step, first_slot, first_target, win_send.at[0, step]))
        copies.append(send(HALF + step, second_slot, second_target, win_send.at[0, HALF + step]))
        for chunk in (2 * step, 2 * step + 1):
            copies.append(send(chunk, whole_slot, whole_target, win_send.at[1, chunk]))
    for chunk in range(CHUNKS):
        copies.append(send(chunk, sibling_slot, sibling, win_send.at[2, chunk]))

    for copy in input_copies:
        copy.wait()

    send_read[...] = jnp.zeros_like(send_read)
    send_read[0:1, 0:CHAN] = readout[...]
    recv_read[pl.ds(my_ch, 1)] = send_read[...][None]

    def to_peers(source, landing, which):
        started = []
        for step in range(1, PEERS):
            peer = lax.rem(my_ch + step, PEERS)
            copy = pltpu.make_async_remote_copy(
                src_ref=source,
                dst_ref=landing,
                send_sem=peer_send.at[which, step],
                recv_sem=peer_recv.at[which, my_ch],
                device_id={"ch": peer},
                device_id_type=MESH,
            )
            copy.start()
            started.append(copy)
        return started

    def from_peers(landing, which):
        for step in range(1, PEERS):
            peer = lax.rem(my_ch + step, PEERS)
            pltpu.make_async_remote_copy(
                src_ref=landing(peer),
                dst_ref=landing(peer),
                send_sem=peer_send.at[which, step],
                recv_sem=peer_recv.at[which, peer],
                device_id={"ch": peer},
                device_id_type=MESH,
            ).wait_recv()

    peer_copies = to_peers(send_read, recv_read.at[my_ch], 4)

    relative = nbr[...] - ATOMS * (me - 2)
    relative = jnp.where(relative < 0, relative + count * ATOMS, relative)
    relative = jnp.where(relative >= count * ATOMS, relative - count * ATOMS, relative)
    relative = jnp.clip(relative, 0, WINDOWS * ATOMS - 1)
    lower = lax.rem(iota((SLOTS, PROBES), 1), 2) == 0
    idx_vmem[...] = relative * 4 + jnp.where(lower, PAD, PAD - 4)
    idx_copies = [
        pltpu.make_async_copy(idx_vmem.at[slot], idx[slot], idx_sem.at[slot])
        for slot in range(SLOTS)
    ]
    for copy in idx_copies:
        copy.start()

    column_comp = iota((96, 512), 1) // CHAN
    row = iota((96, 512), 0)
    spread = (lax.rem(row, 32) == column_comp) & (row < 64)
    expand[:, 0:512] = jnp.where(spread, 1.0, 0.0).astype(bf16)
    radial_rows = jnp.zeros((BASIS, 512), f32)
    comp = iota((CHAN, 512), 1) // CHAN
    same_chan = iota((CHAN, 512), 0) == lax.rem(iota((CHAN, 512), 1), CHAN)
    for degree, (first, last) in enumerate(DEGREES):
        pick = jnp.where(same_chan & (comp >= first) & (comp < last), 1.0, 0.0).astype(bf16)
        for part in split3(radial[degree]):
            radial_rows += dot(part, pick, 1, 0)
    radial_high = radial_rows.astype(bf16).astype(f32)
    radial_low = radial_rows - radial_high
    expand[:, 512:1024] = jnp.concatenate(
        [jnp.zeros((64, 512), f32), radial_high, radial_high, radial_low, radial_low], axis=0
    ).astype(bf16)

    feats[...] = jnp.zeros_like(feats)
    table[0:PAD, :] = jnp.zeros((PAD, 128), f32)
    table[TABLE_ROWS - PAD : TABLE_ROWS, :] = jnp.zeros((PAD, 128), f32)

    def weight_block(step, carry):
        slot0 = pl.multiple_of((step // 4) * 8, 8)
        probe0 = pl.multiple_of(lax.rem(step, 4) * 128, 128)
        where = (pl.ds(slot0, 8), pl.ds(probe0, 128))
        parts, radius_sq = harmonics(disp[(0,) + where], disp[(1,) + where], disp[(2,) + where])
        for comp_index, part in enumerate(parts):
            feats[8 * comp_index : 8 * comp_index + 8, :] = part
        use = mask[where].astype(f32) * (1.0 / SLOTS)
        for basis in range(BASIS):
            away = radius_sq - 0.9 * basis
            feats[256 + 8 * basis : 264 + 8 * basis, :] = jnp.exp(-(away * away)) * use
        for inner in range(8):
            values = feats[pl.ds(inner, 40, stride=8), :]
            high = values.astype(bf16).astype(f32)
            low = values - high
            left = jnp.concatenate(
                [high[0:32], low[0:32], high[32:40], low[32:40], high[32:40], low[32:40]], axis=0
            ).astype(bf16)
            base = probe0 * 4
            for pair in range(2):
                lanes = slice(256 * pair, 256 * pair + 256)
                lanes_radial = slice(512 + 256 * pair, 768 + 256 * pair)
                product = dot(left, expand[:, lanes], 0, 0) * dot(
                    left, expand[:, lanes_radial], 0, 0
                )
                for part in range(2):
                    weights[slot0 + inner, pl.ds(base + 2 * pair + part, 128, stride=4), :] = product[
                        :, 128 * part : 128 * part + 128
                    ]
        return carry

    lax.fori_loop(0, 16, weight_block, 0)

    eye = jnp.where(iota((CHUNK, CHUNK), 0) == iota((CHUNK, CHUNK), 1), 1.0, 0.0).astype(bf16)

    def to_table(slot, chunk):
        base = PAD + (slot * ATOMS + chunk * CHUNK) * 4
        for part in range(4):
            if part < 3:
                block = win[slot, 128 * part : 128 * part + 128, columns(chunk)]
            else:
                block = jnp.concatenate(
                    [win[slot, 384:400, columns(chunk)], jnp.zeros((112, CHUNK), bf16)], axis=0
                )
            table[pl.ds(base + part, CHUNK, stride=4), :] = dot(eye, block, 1, 1)

    def arrived(slot, chunk):
        pltpu.make_async_remote_copy(
            src_ref=win.at[slot, :, columns(chunk)],
            dst_ref=win.at[slot, :, columns(chunk)],
            send_sem=fwd_send.at[0, 0],
            recv_sem=win_recv.at[slot, chunk],
            device_id={"dom": sibling},
            device_id_type=MESH,
        ).wait_recv()

    def forward(chunk, slot_here, slot_there, which, step):
        copy = pltpu.make_async_remote_copy(
            src_ref=win.at[slot_here, :, columns(chunk)],
            dst_ref=win.at[slot_there, :, columns(chunk)],
            send_sem=fwd_send.at[which, step],
            recv_sem=win_recv.at[slot_there, chunk],
            device_id={"dom": sibling},
            device_id_type=MESH,
        )
        copy.start()
        return copy

    own_copy.wait()

    def own_chunk(chunk, carry):
        to_table(2, chunk)
        return carry

    lax.fori_loop(0, CHUNKS, own_chunk, 0)

    def sibling_chunk(chunk, carry):
        arrived(4 - sibling_slot, chunk)
        to_table(4 - sibling_slot, chunk)
        return carry

    lax.fori_loop(0, CHUNKS, sibling_chunk, 0)

    left_here = jnp.where(odd == 1, 0, 1)
    left_there = 1 - left_here
    right_here = jnp.where(odd == 1, 3, 4)
    right_there = 7 - right_here
    whole_here = jnp.where(odd == 1, 4, 0)

    def shared_step(step, carry):
        direct = odd * HALF + step
        arrived(left_here, direct)
        forward(direct, left_here, left_there, 0, step)
        arrived(right_here, direct)
        forward(direct, right_here, right_there, 1, step)
        to_table(left_here, direct)
        to_table(right_here, direct)
        arrived(whole_here, 2 * step)
        to_table(whole_here, 2 * step)
        arrived(whole_here, 2 * step + 1)
        to_table(whole_here, 2 * step + 1)
        other = even_case * HALF + step
        arrived(left_here, other)
        to_table(left_here, other)
        arrived(right_here, other)
        to_table(right_here, other)
        return carry

    lax.fori_loop(0, HALF, shared_step, 0)

    for copy in idx_copies:
        copy.wait()
    upper_half = iota((8, 128), 0) < 4

    def probe_block(block, carry):
        for inner in range(UNROLL):
            pair = block * UNROLL + inner
            first_probe, second_probe = 2 * pair, 2 * pair + 1
            rows_at = pl.ds(pl.multiple_of(pair * 8, 8), 8)
            total = jnp.zeros((8, 128), f32)
            for slot in range(SLOTS):
                first = table[pl.ds(idx[slot][first_probe], 8), :]
                second = table[pl.ds(idx[slot][second_probe], 8), :]
                atom = jnp.where(upper_half, first, second)
                total = total + atom * weights[slot, rows_at, :]
            acc[rows_at, :] = total
        return carry

    chan_pick = jnp.where(
        iota((CHAN, 128), 0) == lax.rem(iota((CHAN, 128), 1), CHAN), 1.0, 0.0
    ).astype(bf16)
    my_rows = pl.ds(pl.multiple_of(my_ch * CHAN, CHAN), CHAN)
    blocks = 64 // UNROLL
    for group in range(4):
        lax.fori_loop(group * blocks, (group + 1) * blocks, probe_block, 0)
        summed = acc[pl.ds(512 * group, 128, stride=4), :]
        for part in range(1, 4):
            summed = summed + acc[pl.ds(512 * group + part, 128, stride=4), :]
        field = jnp.zeros((CHAN, 128), f32)
        for part in split3(summed):
            field = field + dot(chan_pick, part, 1, 1)
        field_all[group, my_rows, :] = field
        tile = field_all.at[group, my_rows, :]
        peer_copies += to_peers(tile, tile, group)

    from_peers(lambda peer: recv_read.at[peer], 4)
    read_row = jnp.zeros((8, 128), f32)
    for peer in range(PEERS):
        part = recv_read[peer]
        read_row = read_row + (part if peer == 0 else pltpu.roll(part, CHAN * peer, 1))
    read_parts = split3(read_row)
    for group in range(4):
        from_peers(
            lambda peer: field_all.at[
                group, pl.ds(pl.multiple_of(peer * CHAN, CHAN), CHAN), :
            ],
            group,
        )
        mixed = jnp.zeros((128, 128), f32)
        for part in split3(field_all[group]):
            mixed = mixed + dot(mixing[...], part, 0, 0)
        active = split3(mixed / (1.0 + jnp.exp(-mixed)))
        dens = jnp.zeros((8, 128), f32)
        for left_part, right_part in ((0, 0), (0, 1), (1, 0), (1, 1), (0, 2), (2, 0)):
            dens = dens + dot(read_parts[left_part], active[right_part], 1, 0)
        out[0:1, 128 * group : 128 * group + 128] = dens[0:1]

    for copy in copies + peer_copies:
        copy.wait_send()

    def forwarded(step, carry):
        for which in range(2):
            pltpu.make_async_remote_copy(
                src_ref=win.at[0, :, columns(0)],
                dst_ref=win.at[0, :, columns(0)],
                send_sem=fwd_send.at[which, step],
                recv_sem=win_recv.at[0, 0],
                device_id={"dom": sibling},
                device_id_type=MESH,
            ).wait_send()
        return carry

    lax.fori_loop(0, HALF, forwarded, 0)


def per_device(feat, nbr, mask, disp, radial, mixing, readout):
    vmem = pl.BlockSpec(memory_space=pltpu.VMEM)
    dma = pltpu.SemaphoreType.DMA
    tile = (8, 128)
    density = pl.pallas_call(
        kernel,
        out_shape=jax.ShapeDtypeStruct((1, PROBES), f32),
        in_specs=[pl.BlockSpec(memory_space=pl.ANY)] * 7,
        out_specs=vmem,
        scratch_shapes=[
            pltpu.VMEM((SLOTS, PROBES), jnp.int32),
            pltpu.VMEM((SLOTS, PROBES), jnp.int32),
            pltpu.VMEM((3, SLOTS, PROBES), f32),
            pltpu.VMEM((5, BASIS, CHAN), f32),
            pltpu.VMEM((128, 128), bf16),
            pltpu.VMEM((1, CHAN), f32),
            pltpu.VMEM((WINDOWS, ROWS, ATOMS), bf16),
            pltpu.VMEM((TABLE_ROWS, 128), f32),
            pltpu.VMEM((SLOTS, SLOT_ROWS, 128), f32),
            pltpu.VMEM((SLOT_ROWS, 128), f32),
            pltpu.VMEM((320, 128), f32),
            pltpu.VMEM((96, 1024), bf16),
            pltpu.VMEM((SLOTS, PROBES), jnp.int32),
            pltpu.VMEM((4, 128, 128), f32),
            pltpu.VMEM(tile, f32),
            pltpu.VMEM((PEERS,) + tile, f32),
            dma((6,)),
            dma((3, CHUNKS)),
            dma((WINDOWS, CHUNKS)),
            dma((2, HALF)),
            dma,
            dma((SLOTS,)),
            dma((5, PEERS)),
            dma((5, PEERS)),
        ]
        + [pltpu.SMEM((PROBES,), jnp.int32)] * SLOTS,
        compiler_params=pltpu.CompilerParams(
            collective_id=0, has_side_effects=True, vmem_limit_bytes=64 * 1024 * 1024 - 65536
        ),
    )(
        feat.reshape(ROWS, ATOMS),
        nbr,
        mask,
        disp,
        radial.transpose(1, 0, 2),
        mixing,
        readout.reshape(1, CHAN),
    )
    return density.reshape(PROBES)


def solution(mesh):
    return jax.shard_map(
        per_device,
        mesh=mesh,
        in_specs=(
            P(None, "ch", "dom"),
            P(None, "dom"),
            P(None, "dom"),
            P(None, None, "dom"),
            P(None, None, "ch"),
            P(),
            P("ch"),
        ),
        out_specs=P("dom"),
        check_vma=False,
    )
```

```python
import functools

import jax
import jax.numpy as jnp
from jax import lax
from jax.experimental import pallas as pl
from jax.experimental.pallas import tpu as pltpu
from jax.sharding import PartitionSpec as P

COMPS = 25
CHAN = 16
ROWS = COMPS * CHAN
ATOMS = 1536
PROBES = 512
SLOTS = 32
BASIS = 8
WINDOWS = 5
CHUNK = 128
CHUNKS = ATOMS // CHUNK
HALF = CHUNKS // 2
PAD = 4
TABLE_ROWS = PAD + WINDOWS * ATOMS * 4 + PAD
SLOT_ROWS = PROBES * 4
PEERS = 8
FAR_FIRST = (4, 3, 5, 2, 6, 1, 7)
UNROLL = 4
DEGREES = ((0, 1), (1, 4), (4, 9), (9, 16), (16, 25))
MESH = pl.DeviceIdType.MESH
f32 = jnp.float32
bf16 = jnp.bfloat16


def harmonics(coord_x, coord_y, coord_z):
    square_x = coord_x * coord_x
    square_y = coord_y * coord_y
    square_z = coord_z * coord_z
    radius_sq = square_x + square_y + square_z
    components = [
        jnp.ones_like(coord_x),
        coord_x,
        coord_y,
        coord_z,
        coord_x * coord_y,
        coord_y * coord_z,
        (3.0 * square_z - radius_sq) * 0.2887,
        coord_x * coord_z,
        0.5 * (square_x - square_y),
        coord_y * (3.0 * square_x - square_y) * 0.2,
        coord_x * coord_y * coord_z,
        coord_y * (4.0 * square_z - square_x - square_y) * 0.15,
        coord_z * (2.0 * square_z - 3.0 * square_x - 3.0 * square_y) * 0.15,
        coord_x * (4.0 * square_z - square_x - square_y) * 0.15,
        0.5 * coord_z * (square_x - square_y),
        coord_x * (square_x - 3.0 * square_y) * 0.2,
        coord_x * coord_y * (square_x - square_y) * 0.5,
        coord_y * coord_z * (3.0 * square_x - square_y) * 0.2,
        coord_x * coord_y * (7.0 * square_z - radius_sq) * 0.1,
        coord_y * coord_z * (7.0 * square_z - 3.0 * radius_sq) * 0.1,
        (35.0 * square_z * square_z - 30.0 * square_z * radius_sq + 3.0 * radius_sq * radius_sq)
        * 0.02,
        coord_x * coord_z * (7.0 * square_z - 3.0 * radius_sq) * 0.1,
        (square_x - square_y) * (7.0 * square_z - radius_sq) * 0.05,
        coord_x * coord_z * (square_x - 3.0 * square_y) * 0.2,
        (square_x * square_x - 6.0 * square_x * square_y + square_y * square_y) * 0.1,
    ]
    return components, radius_sq


def iota(shape, dim):
    return lax.broadcasted_iota(jnp.int32, shape, dim)


def split3(value):
    first = value.astype(bf16)
    rest = value - first.astype(f32)
    second = rest.astype(bf16)
    third = (rest - second.astype(f32)).astype(bf16)
    return first, second, third


def dot(left, right, left_dim, right_dim):
    return lax.dot_general(
        left, right, (((left_dim,), (right_dim,)), ((), ())), preferred_element_type=f32
    )


def kernel(
    feat,
    nbr_hbm,
    mask_hbm,
    disp_hbm,
    radial_hbm,
    mixing_hbm,
    readout_hbm,
    out,
    nbr,
    mask,
    disp,
    radial,
    mixing,
    readout,
    win,
    table,
    weights,
    acc,
    feats,
    expand,
    idx_vmem,
    field_all,
    send_read,
    recv_read,
    input_sem,
    win_send,
    win_recv,
    fwd_send,
    own_sem,
    idx_sem,
    peer_send,
    peer_recv,
    *idx,
):
    me = lax.axis_index("dom")
    my_ch = lax.axis_index("ch")
    count = lax.axis_size("dom")
    odd = lax.rem(me, 2)

    def at(offset):
        return lax.rem(me + offset + count, count)

    barrier = pltpu.get_barrier_semaphore()
    for offset in (-2, -1, 1, 2):
        pl.semaphore_signal(barrier, inc=1, device_id={"dom": at(offset)}, device_id_type=MESH)
    for step in FAR_FIRST:
        peer = lax.rem(my_ch + step, PEERS)
        pl.semaphore_signal(barrier, inc=1, device_id={"ch": peer}, device_id_type=MESH)

    input_copies = [
        pltpu.make_async_copy(source, landing, input_sem.at[place])
        for place, (source, landing) in enumerate(
            (
                (nbr_hbm, nbr),
                (mask_hbm, mask),
                (disp_hbm, disp),
                (radial_hbm, radial),
                (mixing_hbm, mixing),
                (readout_hbm, readout),
            )
        )
    ]
    for copy in input_copies:
        copy.start()
    own_copy = pltpu.make_async_copy(feat, win.at[2], own_sem)
    own_copy.start()
    pl.semaphore_wait(barrier, 4 + PEERS - 1)

    def columns(chunk):
        return pl.ds(pl.multiple_of(chunk * CHUNK, CHUNK), CHUNK)

    def send(chunk, slot, target, sems):
        copy = pltpu.make_async_remote_copy(
            src_ref=feat.at[:, columns(chunk)],
            dst_ref=win.at[slot, :, columns(chunk)],
            send_sem=sems,
            recv_sem=win_recv.at[slot, chunk],
            device_id={"dom": target},
            device_id_type=MESH,
        )
        copy.start()
        return copy

    even_case = 1 - odd
    first_target = jnp.where(odd == 1, at(1), at(-2))
    first_slot = jnp.where(odd == 1, 1, 4)
    second_target = jnp.where(odd == 1, at(2), at(-1))
    second_slot = jnp.where(odd == 1, 0, 3)
    whole_target = jnp.where(odd == 1, at(-2), at(2))
    whole_slot = jnp.where(odd == 1, 4, 0)
    sibling = jnp.where(odd == 1, at(-1), at(1))
    sibling_slot = jnp.where(odd == 1, 3, 1)

    copies = []
    for step in range(HALF):
        copies.append(send(step, first_slot, first_target, win_send.at[0, step]))
        copies.append(send(HALF + step, second_slot, second_target, win_send.at[0, HALF + step]))
    for chunk in range(CHUNKS):
        copies.append(send(chunk, sibling_slot, sibling, win_send.at[2, chunk]))

    for copy in input_copies:
        copy.wait()

    send_read[...] = jnp.zeros_like(send_read)
    send_read[0:1, 0:CHAN] = readout[...]
    recv_read[pl.ds(my_ch, 1)] = send_read[...][None]

    def to_peers(source, landing, which):
        started = []
        for step in FAR_FIRST:
            peer = lax.rem(my_ch + step, PEERS)
            copy = pltpu.make_async_remote_copy(
                src_ref=source,
                dst_ref=landing,
                send_sem=peer_send.at[which, step],
                recv_sem=peer_recv.at[which, my_ch],
                device_id={"ch": peer},
                device_id_type=MESH,
            )
            copy.start()
            started.append(copy)
        return started

    def from_peers(landing, which):
        for step in range(1, PEERS):
            peer = lax.rem(my_ch + step, PEERS)
            pltpu.make_async_remote_copy(
                src_ref=landing(peer),
                dst_ref=landing(peer),
                send_sem=peer_send.at[which, step],
                recv_sem=peer_recv.at[which, peer],
                device_id={"ch": peer},
                device_id_type=MESH,
            ).wait_recv()

    peer_copies = to_peers(send_read, recv_read.at[my_ch], 4)

    relative = nbr[...] - ATOMS * (me - 2)
    relative = jnp.where(relative < 0, relative + count * ATOMS, relative)
    relative = jnp.where(relative >= count * ATOMS, relative - count * ATOMS, relative)
    relative = jnp.clip(relative, 0, WINDOWS * ATOMS - 1)
    lower = lax.rem(iota((SLOTS, PROBES), 1), 2) == 0
    idx_vmem[...] = relative * 4 + jnp.where(lower, PAD, PAD - 4)
    idx_copies = [
        pltpu.make_async_copy(idx_vmem.at[slot], idx[slot], idx_sem.at[slot])
        for slot in range(SLOTS)
    ]
    for copy in idx_copies:
        copy.start()

    column_comp = iota((96, 512), 1) // CHAN
    row = iota((96, 512), 0)
    spread = (lax.rem(row, 32) == column_comp) & (row < 64)
    expand[:, 0:512] = jnp.where(spread, 1.0, 0.0).astype(bf16)
    radial_rows = jnp.zeros((BASIS, 512), f32)
    comp = iota((CHAN, 512), 1) // CHAN
    same_chan = iota((CHAN, 512), 0) == lax.rem(iota((CHAN, 512), 1), CHAN)
    for degree, (first, last) in enumerate(DEGREES):
        pick = jnp.where(same_chan & (comp >= first) & (comp < last), 1.0, 0.0).astype(bf16)
        for part in split3(radial[degree]):
            radial_rows += dot(part, pick, 1, 0)
    radial_high = radial_rows.astype(bf16).astype(f32)
    radial_low = radial_rows - radial_high
    expand[:, 512:1024] = jnp.concatenate(
        [jnp.zeros((64, 512), f32), radial_high, radial_high, radial_low, radial_low], axis=0
    ).astype(bf16)

    feats[...] = jnp.zeros_like(feats)
    table[0:PAD, :] = jnp.zeros((PAD, 128), f32)
    table[TABLE_ROWS - PAD : TABLE_ROWS, :] = jnp.zeros((PAD, 128), f32)

    def weight_block(step, carry):
        slot0 = pl.multiple_of((step // 4) * 8, 8)
        probe0 = pl.multiple_of(lax.rem(step, 4) * 128, 128)
        where = (pl.ds(slot0, 8), pl.ds(probe0, 128))
        parts, radius_sq = harmonics(disp[(0,) + where], disp[(1,) + where], disp[(2,) + where])
        for comp_index, part in enumerate(parts):
            feats[8 * comp_index : 8 * comp_index + 8, :] = part
        use = mask[where].astype(f32) * (1.0 / SLOTS)
        for basis in range(BASIS):
            away = radius_sq - 0.9 * basis
            feats[256 + 8 * basis : 264 + 8 * basis, :] = jnp.exp(-(away * away)) * use
        for inner in range(8):
            values = feats[pl.ds(inner, 40, stride=8), :]
            high = values.astype(bf16).astype(f32)
            low = values - high
            left = jnp.concatenate(
                [high[0:32], low[0:32], high[32:40], low[32:40], high[32:40], low[32:40]], axis=0
            ).astype(bf16)
            base = probe0 * 4
            for pair in range(2):
                lanes = slice(256 * pair, 256 * pair + 256)
                lanes_radial = slice(512 + 256 * pair, 768 + 256 * pair)
                product = dot(left, expand[:, lanes], 0, 0) * dot(
                    left, expand[:, lanes_radial], 0, 0
                )
                for part in range(2):
                    weights[slot0 + inner, pl.ds(base + 2 * pair + part, 128, stride=4), :] = product[
                        :, 128 * part : 128 * part + 128
                    ]
        return carry

    lax.fori_loop(0, 6, weight_block, 0)

    for chunk in range(CHUNKS):
        copies.append(send(chunk, whole_slot, whole_target, win_send.at[1, chunk]))

    lax.fori_loop(6, 16, weight_block, 0)

    eye = jnp.where(iota((CHUNK, CHUNK), 0) == iota((CHUNK, CHUNK), 1), 1.0, 0.0).astype(bf16)

    def to_table(slot, chunk):
        base = PAD + (slot * ATOMS + chunk * CHUNK) * 4
        for part in range(4):
            if part < 3:
                block = win[slot, 128 * part : 128 * part + 128, columns(chunk)]
            else:
                block = jnp.concatenate(
                    [win[slot, 384:400, columns(chunk)], jnp.zeros((112, CHUNK), bf16)], axis=0
                )
            table[pl.ds(base + part, CHUNK, stride=4), :] = dot(eye, block, 1, 1)

    def arrived(slot, chunk):
        pltpu.make_async_remote_copy(
            src_ref=win.at[slot, :, columns(chunk)],
            dst_ref=win.at[slot, :, columns(chunk)],
            send_sem=fwd_send.at[0, 0],
            recv_sem=win_recv.at[slot, chunk],
            device_id={"dom": sibling},
            device_id_type=MESH,
        ).wait_recv()

    def forward(chunk, slot_here, slot_there, which, step):
        copy = pltpu.make_async_remote_copy(
            src_ref=win.at[slot_here, :, columns(chunk)],
            dst_ref=win.at[slot_there, :, columns(chunk)],
            send_sem=fwd_send.at[which, step],
            recv_sem=win_recv.at[slot_there, chunk],
            device_id={"dom": sibling},
            device_id_type=MESH,
        )
        copy.start()
        return copy

    own_copy.wait()

    def own_chunk(chunk, carry):
        to_table(2, chunk)
        return carry

    lax.fori_loop(0, CHUNKS, own_chunk, 0)

    def sibling_chunk(chunk, carry):
        arrived(4 - sibling_slot, chunk)
        to_table(4 - sibling_slot, chunk)
        return carry

    lax.fori_loop(0, CHUNKS, sibling_chunk, 0)

    left_here = jnp.where(odd == 1, 0, 1)
    left_there = 1 - left_here
    right_here = jnp.where(odd == 1, 3, 4)
    right_there = 7 - right_here
    whole_here = jnp.where(odd == 1, 4, 0)

    def shared_step(step, carry):
        direct = odd * HALF + step
        arrived(left_here, direct)
        forward(direct, left_here, left_there, 0, step)
        arrived(right_here, direct)
        forward(direct, right_here, right_there, 1, step)
        to_table(left_here, direct)
        to_table(right_here, direct)
        other = even_case * HALF + step
        arrived(left_here, other)
        to_table(left_here, other)
        arrived(right_here, other)
        to_table(right_here, other)
        return carry

    lax.fori_loop(0, HALF, shared_step, 0)

    def whole_step(chunk, carry):
        arrived(whole_here, chunk)
        to_table(whole_here, chunk)
        return carry

    lax.fori_loop(0, CHUNKS, whole_step, 0)

    for copy in idx_copies:
        copy.wait()
    upper_half = iota((8, 128), 0) < 4

    def probe_block(block, carry):
        for inner in range(UNROLL):
            pair = block * UNROLL + inner
            first_probe, second_probe = 2 * pair, 2 * pair + 1
            rows_at = pl.ds(pl.multiple_of(pair * 8, 8), 8)
            total = jnp.zeros((8, 128), f32)
            for slot in range(SLOTS):
                first = table[pl.ds(idx[slot][first_probe], 8), :]
                second = table[pl.ds(idx[slot][second_probe], 8), :]
                atom = jnp.where(upper_half, first, second)
                total = total + atom * weights[slot, rows_at, :]
            acc[rows_at, :] = total
        return carry

    chan_pick = jnp.where(
        iota((CHAN, 128), 0) == lax.rem(iota((CHAN, 128), 1), CHAN), 1.0, 0.0
    ).astype(bf16)
    my_rows = pl.ds(pl.multiple_of(my_ch * CHAN, CHAN), CHAN)
    blocks = 64 // UNROLL

    def probe_group(group, carry):
        lax.fori_loop(group * blocks, (group + 1) * blocks, probe_block, 0)
        start = group * 512
        summed = acc[pl.ds(start, 128, stride=4), :]
        for part in range(1, 4):
            summed = summed + acc[pl.ds(start + part, 128, stride=4), :]
        field = jnp.zeros((CHAN, 128), f32)
        for part in split3(summed):
            field = field + dot(chan_pick, part, 1, 1)
        field_all[group, my_rows, :] = field
        tile = field_all.at[group, my_rows, :]
        to_peers(tile, tile, group)
        return carry

    lax.fori_loop(0, 4, probe_group, 0)

    for copy in copies + peer_copies:
        copy.wait_send()

    def forwarded(step, carry):
        for which in range(2):
            pltpu.make_async_remote_copy(
                src_ref=win.at[0, :, columns(0)],
                dst_ref=win.at[0, :, columns(0)],
                send_sem=fwd_send.at[which, step],
                recv_sem=win_recv.at[0, 0],
                device_id={"dom": sibling},
                device_id_type=MESH,
            ).wait_send()
        return carry

    lax.fori_loop(0, HALF, forwarded, 0)

    def sent(group, carry):
        tile = field_all.at[group, my_rows, :]
        for step in range(1, PEERS):
            pltpu.make_async_remote_copy(
                src_ref=tile,
                dst_ref=tile,
                send_sem=peer_send.at[group, step],
                recv_sem=peer_recv.at[group, my_ch],
                device_id={"ch": lax.rem(my_ch + step, PEERS)},
                device_id_type=MESH,
            ).wait_send()
        return carry

    lax.fori_loop(0, 4, sent, 0)

    from_peers(lambda peer: recv_read.at[peer], 4)
    read_row = jnp.zeros((8, 128), f32)
    for peer in range(PEERS):
        part = recv_read[peer]
        read_row = read_row + (part if peer == 0 else pltpu.roll(part, CHAN * peer, 1))
    read_parts = split3(read_row)
    for group in range(4):
        from_peers(
            lambda peer: field_all.at[
                group, pl.ds(pl.multiple_of(peer * CHAN, CHAN), CHAN), :
            ],
            group,
        )
        mixed = jnp.zeros((128, 128), f32)
        for part in split3(field_all[group]):
            mixed = mixed + dot(mixing[...], part, 0, 0)
        active = split3(mixed / (1.0 + jnp.exp(-mixed)))
        dens = jnp.zeros((8, 128), f32)
        for left_part, right_part in ((0, 0), (0, 1), (1, 0), (1, 1), (0, 2), (2, 0)):
            dens = dens + dot(read_parts[left_part], active[right_part], 1, 0)
        out[0:1, 128 * group : 128 * group + 128] = dens[0:1]


def per_device(feat, nbr, mask, disp, radial, mixing, readout):
    vmem = pl.BlockSpec(memory_space=pltpu.VMEM)
    dma = pltpu.SemaphoreType.DMA
    tile = (8, 128)
    density = pl.pallas_call(
        kernel,
        out_shape=jax.ShapeDtypeStruct((1, PROBES), f32),
        in_specs=[pl.BlockSpec(memory_space=pl.ANY)] * 7,
        out_specs=vmem,
        scratch_shapes=[
            pltpu.VMEM((SLOTS, PROBES), jnp.int32),
            pltpu.VMEM((SLOTS, PROBES), jnp.int32),
            pltpu.VMEM((3, SLOTS, PROBES), f32),
            pltpu.VMEM((5, BASIS, CHAN), f32),
            pltpu.VMEM((128, 128), bf16),
            pltpu.VMEM((1, CHAN), f32),
            pltpu.VMEM((WINDOWS, ROWS, ATOMS), bf16),
            pltpu.VMEM((TABLE_ROWS, 128), f32),
            pltpu.VMEM((SLOTS, SLOT_ROWS, 128), f32),
            pltpu.VMEM((SLOT_ROWS, 128), f32),
            pltpu.VMEM((320, 128), f32),
            pltpu.VMEM((96, 1024), bf16),
            pltpu.VMEM((SLOTS, PROBES), jnp.int32),
            pltpu.VMEM((4, 128, 128), f32),
            pltpu.VMEM(tile, f32),
            pltpu.VMEM((PEERS,) + tile, f32),
            dma((6,)),
            dma((3, CHUNKS)),
            dma((WINDOWS, CHUNKS)),
            dma((2, HALF)),
            dma,
            dma((SLOTS,)),
            dma((5, PEERS)),
            dma((5, PEERS)),
        ]
        + [pltpu.SMEM((PROBES,), jnp.int32)] * SLOTS,
        compiler_params=pltpu.CompilerParams(
            collective_id=0, has_side_effects=True, vmem_limit_bytes=64 * 1024 * 1024 - 65536
        ),
    )(
        feat.reshape(ROWS, ATOMS),
        nbr,
        mask,
        disp,
        radial.transpose(1, 0, 2),
        mixing,
        readout.reshape(1, CHAN),
    )
    return density.reshape(PROBES)


def solution(mesh):
    return jax.shard_map(
        per_device,
        mesh=mesh,
        in_specs=(
            P(None, "ch", "dom"),
            P(None, "dom"),
            P(None, "dom"),
            P(None, None, "dom"),
            P(None, None, "ch"),
            P(),
            P("ch"),
        ),
        out_specs=P("dom"),
        check_vma=False,
    )
```

```python
import functools

import jax
import jax.numpy as jnp
from jax import lax
from jax.experimental import pallas as pl
from jax.experimental.pallas import tpu as pltpu
from jax.sharding import PartitionSpec as P

COMPS = 25
CHAN = 16
ROWS = COMPS * CHAN
ATOMS = 1536
PROBES = 512
SLOTS = 32
BASIS = 8
WINDOWS = 5
CHUNK = 128
CHUNKS = ATOMS // CHUNK
PAD = 4
TABLE_ROWS = PAD + WINDOWS * ATOMS * 4 + PAD
SLOT_ROWS = PROBES * 4
PEERS = 8
FAR_FIRST = (4, 3, 5, 2, 6, 1, 7)
UNROLL = 4
DEGREES = ((0, 1), (1, 4), (4, 9), (9, 16), (16, 25))
MESH = pl.DeviceIdType.MESH
f32 = jnp.float32
bf16 = jnp.bfloat16


def harmonics(coord_x, coord_y, coord_z):
    square_x = coord_x * coord_x
    square_y = coord_y * coord_y
    square_z = coord_z * coord_z
    radius_sq = square_x + square_y + square_z
    components = [
        jnp.ones_like(coord_x),
        coord_x,
        coord_y,
        coord_z,
        coord_x * coord_y,
        coord_y * coord_z,
        (3.0 * square_z - radius_sq) * 0.2887,
        coord_x * coord_z,
        0.5 * (square_x - square_y),
        coord_y * (3.0 * square_x - square_y) * 0.2,
        coord_x * coord_y * coord_z,
        coord_y * (4.0 * square_z - square_x - square_y) * 0.15,
        coord_z * (2.0 * square_z - 3.0 * square_x - 3.0 * square_y) * 0.15,
        coord_x * (4.0 * square_z - square_x - square_y) * 0.15,
        0.5 * coord_z * (square_x - square_y),
        coord_x * (square_x - 3.0 * square_y) * 0.2,
        coord_x * coord_y * (square_x - square_y) * 0.5,
        coord_y * coord_z * (3.0 * square_x - square_y) * 0.2,
        coord_x * coord_y * (7.0 * square_z - radius_sq) * 0.1,
        coord_y * coord_z * (7.0 * square_z - 3.0 * radius_sq) * 0.1,
        (35.0 * square_z * square_z - 30.0 * square_z * radius_sq + 3.0 * radius_sq * radius_sq)
        * 0.02,
        coord_x * coord_z * (7.0 * square_z - 3.0 * radius_sq) * 0.1,
        (square_x - square_y) * (7.0 * square_z - radius_sq) * 0.05,
        coord_x * coord_z * (square_x - 3.0 * square_y) * 0.2,
        (square_x * square_x - 6.0 * square_x * square_y + square_y * square_y) * 0.1,
    ]
    return components, radius_sq


def iota(shape, dim):
    return lax.broadcasted_iota(jnp.int32, shape, dim)


def split3(value):
    first = value.astype(bf16)
    rest = value - first.astype(f32)
    second = rest.astype(bf16)
    third = (rest - second.astype(f32)).astype(bf16)
    return first, second, third


def dot(left, right, left_dim, right_dim):
    return lax.dot_general(
        left, right, (((left_dim,), (right_dim,)), ((), ())), preferred_element_type=f32
    )


def kernel(
    feat,
    nbr_hbm,
    mask_hbm,
    disp_hbm,
    radial_hbm,
    mixing_hbm,
    readout_hbm,
    out,
    nbr,
    mask,
    disp,
    radial,
    mixing,
    readout,
    win,
    table,
    weights,
    acc,
    feats,
    expand,
    idx_vmem,
    field_all,
    send_read,
    recv_read,
    input_sem,
    win_send,
    win_recv,
    fwd_send,
    own_sem,
    idx_sem,
    peer_send,
    peer_recv,
    *idx,
):
    me = lax.axis_index("dom")
    my_ch = lax.axis_index("ch")
    count = lax.axis_size("dom")
    odd = lax.rem(me, 2)

    def at(offset):
        return lax.rem(me + offset + count, count)

    barrier = pltpu.get_barrier_semaphore()
    for offset in (-2, -1, 1, 2):
        pl.semaphore_signal(barrier, inc=1, device_id={"dom": at(offset)}, device_id_type=MESH)
    for step in FAR_FIRST:
        peer = lax.rem(my_ch + step, PEERS)
        pl.semaphore_signal(barrier, inc=1, device_id={"ch": peer}, device_id_type=MESH)

    input_copies = [
        pltpu.make_async_copy(source, landing, input_sem.at[place])
        for place, (source, landing) in enumerate(
            (
                (nbr_hbm, nbr),
                (mask_hbm, mask),
                (disp_hbm, disp),
                (radial_hbm, radial),
                (mixing_hbm, mixing),
                (readout_hbm, readout),
            )
        )
    ]
    for copy in input_copies:
        copy.start()
    own_copy = pltpu.make_async_copy(feat, win.at[2], own_sem)
    own_copy.start()
    pl.semaphore_wait(barrier, 4 + PEERS - 1)

    def columns(chunk):
        return pl.ds(pl.multiple_of(chunk * CHUNK, CHUNK), CHUNK)

    def send(chunk, slot, target, sems):
        copy = pltpu.make_async_remote_copy(
            src_ref=feat.at[:, columns(chunk)],
            dst_ref=win.at[slot, :, columns(chunk)],
            send_sem=sems,
            recv_sem=win_recv.at[slot, chunk],
            device_id={"dom": target},
            device_id_type=MESH,
        )
        copy.start()
        return copy

    shared_target = jnp.where(odd == 1, at(2), at(-2))
    shared_slot = jnp.where(odd == 1, 0, 4)
    whole_target = jnp.where(odd == 1, at(-2), at(2))
    whole_slot = jnp.where(odd == 1, 4, 0)
    sibling = jnp.where(odd == 1, at(-1), at(1))
    sibling_slot = jnp.where(odd == 1, 3, 1)

    copies = []
    for chunk in range(CHUNKS):
        copies.append(send(chunk, shared_slot, shared_target, win_send.at[0, chunk]))
    for chunk in range(CHUNKS):
        copies.append(send(chunk, sibling_slot, sibling, win_send.at[2, chunk]))

    for copy in input_copies:
        copy.wait()

    send_read[...] = jnp.zeros_like(send_read)
    send_read[0:1, 0:CHAN] = readout[...]
    recv_read[pl.ds(my_ch, 1)] = send_read[...][None]

    def to_peers(source, landing, which):
        started = []
        for step in FAR_FIRST:
            peer = lax.rem(my_ch + step, PEERS)
            copy = pltpu.make_async_remote_copy(
                src_ref=source,
                dst_ref=landing,
                send_sem=peer_send.at[which, step],
                recv_sem=peer_recv.at[which, my_ch],
                device_id={"ch": peer},
                device_id_type=MESH,
            )
            copy.start()
            started.append(copy)
        return started

    def from_peers(landing, which):
        for step in range(1, PEERS):
            peer = lax.rem(my_ch + step, PEERS)
            pltpu.make_async_remote_copy(
                src_ref=landing(peer),
                dst_ref=landing(peer),
                send_sem=peer_send.at[which, step],
                recv_sem=peer_recv.at[which, peer],
                device_id={"ch": peer},
                device_id_type=MESH,
            ).wait_recv()

    peer_copies = to_peers(send_read, recv_read.at[my_ch], 4)

    relative = nbr[...] - ATOMS * (me - 2)
    relative = jnp.where(relative < 0, relative + count * ATOMS, relative)
    relative = jnp.where(relative >= count * ATOMS, relative - count * ATOMS, relative)
    relative = jnp.clip(relative, 0, WINDOWS * ATOMS - 1)
    lower = lax.rem(iota((SLOTS, PROBES), 1), 2) == 0
    idx_vmem[...] = relative * 4 + jnp.where(lower, PAD, PAD - 4)
    idx_copies = [
        pltpu.make_async_copy(idx_vmem.at[slot], idx[slot], idx_sem.at[slot])
        for slot in range(SLOTS)
    ]
    for copy in idx_copies:
        copy.start()

    column_comp = iota((96, 512), 1) // CHAN
    row = iota((96, 512), 0)
    spread = (lax.rem(row, 32) == column_comp) & (row < 64)
    expand[:, 0:512] = jnp.where(spread, 1.0, 0.0).astype(bf16)
    radial_rows = jnp.zeros((BASIS, 512), f32)
    comp = iota((CHAN, 512), 1) // CHAN
    same_chan = iota((CHAN, 512), 0) == lax.rem(iota((CHAN, 512), 1), CHAN)
    for degree, (first, last) in enumerate(DEGREES):
        pick = jnp.where(same_chan & (comp >= first) & (comp < last), 1.0, 0.0).astype(bf16)
        for part in split3(radial[degree]):
            radial_rows += dot(part, pick, 1, 0)
    radial_high = radial_rows.astype(bf16).astype(f32)
    radial_low = radial_rows - radial_high
    expand[:, 512:1024] = jnp.concatenate(
        [jnp.zeros((64, 512), f32), radial_high, radial_high, radial_low, radial_low], axis=0
    ).astype(bf16)

    feats[...] = jnp.zeros_like(feats)
    table[0:PAD, :] = jnp.zeros((PAD, 128), f32)
    table[TABLE_ROWS - PAD : TABLE_ROWS, :] = jnp.zeros((PAD, 128), f32)

    def weight_block(step, carry):
        slot0 = pl.multiple_of((step // 4) * 8, 8)
        probe0 = pl.multiple_of(lax.rem(step, 4) * 128, 128)
        where = (pl.ds(slot0, 8), pl.ds(probe0, 128))
        parts, radius_sq = harmonics(disp[(0,) + where], disp[(1,) + where], disp[(2,) + where])
        for comp_index, part in enumerate(parts):
            feats[8 * comp_index : 8 * comp_index + 8, :] = part
        use = mask[where].astype(f32) * (1.0 / SLOTS)
        for basis in range(BASIS):
            away = radius_sq - 0.9 * basis
            feats[256 + 8 * basis : 264 + 8 * basis, :] = jnp.exp(-(away * away)) * use
        for inner in range(8):
            values = feats[pl.ds(inner, 40, stride=8), :]
            high = values.astype(bf16).astype(f32)
            low = values - high
            left = jnp.concatenate(
                [high[0:32], low[0:32], high[32:40], low[32:40], high[32:40], low[32:40]], axis=0
            ).astype(bf16)
            base = probe0 * 4
            for pair in range(2):
                lanes = slice(256 * pair, 256 * pair + 256)
                lanes_radial = slice(512 + 256 * pair, 768 + 256 * pair)
                product = dot(left, expand[:, lanes], 0, 0) * dot(
                    left, expand[:, lanes_radial], 0, 0
                )
                for part in range(2):
                    weights[slot0 + inner, pl.ds(base + 2 * pair + part, 128, stride=4), :] = product[
                        :, 128 * part : 128 * part + 128
                    ]
        return carry

    lax.fori_loop(0, 8, weight_block, 0)

    for chunk in range(CHUNKS):
        copies.append(send(chunk, whole_slot, whole_target, win_send.at[1, chunk]))

    lax.fori_loop(8, 16, weight_block, 0)

    eye = jnp.where(iota((CHUNK, CHUNK), 0) == iota((CHUNK, CHUNK), 1), 1.0, 0.0).astype(bf16)

    def to_table(slot, chunk):
        base = PAD + (slot * ATOMS + chunk * CHUNK) * 4
        for part in range(4):
            if part < 3:
                block = win[slot, 128 * part : 128 * part + 128, columns(chunk)]
            else:
                block = jnp.concatenate(
                    [win[slot, 384:400, columns(chunk)], jnp.zeros((112, CHUNK), bf16)], axis=0
                )
            table[pl.ds(base + part, CHUNK, stride=4), :] = dot(eye, block, 1, 1)

    def arrived(slot, chunk):
        pltpu.make_async_remote_copy(
            src_ref=win.at[slot, :, columns(chunk)],
            dst_ref=win.at[slot, :, columns(chunk)],
            send_sem=fwd_send.at[0],
            recv_sem=win_recv.at[slot, chunk],
            device_id={"dom": sibling},
            device_id_type=MESH,
        ).wait_recv()

    def forward(chunk, slot_here, slot_there):
        copy = pltpu.make_async_remote_copy(
            src_ref=win.at[slot_here, :, columns(chunk)],
            dst_ref=win.at[slot_there, :, columns(chunk)],
            send_sem=fwd_send.at[chunk],
            recv_sem=win_recv.at[slot_there, chunk],
            device_id={"dom": sibling},
            device_id_type=MESH,
        )
        copy.start()
        return copy

    own_copy.wait()

    def own_chunk(chunk, carry):
        to_table(2, chunk)
        return carry

    lax.fori_loop(0, CHUNKS, own_chunk, 0)

    def sibling_chunk(chunk, carry):
        arrived(4 - sibling_slot, chunk)
        to_table(4 - sibling_slot, chunk)
        return carry

    lax.fori_loop(0, CHUNKS, sibling_chunk, 0)

    handed_slot = jnp.where(odd == 1, 1, 3)
    gotten_slot = jnp.where(odd == 1, 3, 1)
    whole_here = jnp.where(odd == 1, 4, 0)

    def shared_step(chunk, carry):
        arrived(shared_slot, chunk)
        forward(chunk, shared_slot, handed_slot)
        to_table(shared_slot, chunk)
        return carry

    lax.fori_loop(0, CHUNKS, shared_step, 0)

    def gotten_step(chunk, carry):
        arrived(gotten_slot, chunk)
        to_table(gotten_slot, chunk)
        return carry

    lax.fori_loop(0, CHUNKS, gotten_step, 0)

    def whole_step(chunk, carry):
        arrived(whole_here, chunk)
        to_table(whole_here, chunk)
        return carry

    lax.fori_loop(0, CHUNKS, whole_step, 0)

    for copy in idx_copies:
        copy.wait()
    upper_half = iota((8, 128), 0) < 4

    def probe_block(block, carry):
        for inner in range(UNROLL):
            pair = block * UNROLL + inner
            first_probe, second_probe = 2 * pair, 2 * pair + 1
            rows_at = pl.ds(pl.multiple_of(pair * 8, 8), 8)
            total = jnp.zeros((8, 128), f32)
            for slot in range(SLOTS):
                first = table[pl.ds(idx[slot][first_probe], 8), :]
                second = table[pl.ds(idx[slot][second_probe], 8), :]
                atom = jnp.where(upper_half, first, second)
                total = total + atom * weights[slot, rows_at, :]
            acc[rows_at, :] = total
        return carry

    chan_pick = jnp.where(
        iota((CHAN, 128), 0) == lax.rem(iota((CHAN, 128), 1), CHAN), 1.0, 0.0
    ).astype(bf16)
    my_rows = pl.ds(pl.multiple_of(my_ch * CHAN, CHAN), CHAN)
    blocks = 64 // UNROLL

    def probe_group(group, carry):
        lax.fori_loop(group * blocks, (group + 1) * blocks, probe_block, 0)
        start = group * 512
        summed = acc[pl.ds(start, 128, stride=4), :]
        for part in range(1, 4):
            summed = summed + acc[pl.ds(start + part, 128, stride=4), :]
        field = jnp.zeros((CHAN, 128), f32)
        for part in split3(summed):
            field = field + dot(chan_pick, part, 1, 1)
        field_all[group, my_rows, :] = field
        tile = field_all.at[group, my_rows, :]
        to_peers(tile, tile, group)
        return carry

    lax.fori_loop(0, 4, probe_group, 0)

    for copy in copies + peer_copies:
        copy.wait_send()

    def forwarded(chunk, carry):
        pltpu.make_async_remote_copy(
            src_ref=win.at[0, :, columns(0)],
            dst_ref=win.at[0, :, columns(0)],
            send_sem=fwd_send.at[chunk],
            recv_sem=win_recv.at[0, 0],
            device_id={"dom": sibling},
            device_id_type=MESH,
        ).wait_send()
        return carry

    lax.fori_loop(0, CHUNKS, forwarded, 0)

    def sent(group, carry):
        tile = field_all.at[group, my_rows, :]
        for step in range(1, PEERS):
            pltpu.make_async_remote_copy(
                src_ref=tile,
                dst_ref=tile,
                send_sem=peer_send.at[group, step],
                recv_sem=peer_recv.at[group, my_ch],
                device_id={"ch": lax.rem(my_ch + step, PEERS)},
                device_id_type=MESH,
            ).wait_send()
        return carry

    lax.fori_loop(0, 4, sent, 0)

    from_peers(lambda peer: recv_read.at[peer], 4)
    read_row = jnp.zeros((8, 128), f32)
    for peer in range(PEERS):
        part = recv_read[peer]
        read_row = read_row + (part if peer == 0 else pltpu.roll(part, CHAN * peer, 1))
    read_parts = split3(read_row)
    for group in range(4):
        from_peers(
            lambda peer: field_all.at[
                group, pl.ds(pl.multiple_of(peer * CHAN, CHAN), CHAN), :
            ],
            group,
        )
        mixed = jnp.zeros((128, 128), f32)
        for part in split3(field_all[group]):
            mixed = mixed + dot(mixing[...], part, 0, 0)
        active = split3(mixed / (1.0 + jnp.exp(-mixed)))
        dens = jnp.zeros((8, 128), f32)
        for left_part, right_part in ((0, 0), (0, 1), (1, 0), (1, 1), (0, 2), (2, 0)):
            dens = dens + dot(read_parts[left_part], active[right_part], 1, 0)
        out[0:1, 128 * group : 128 * group + 128] = dens[0:1]


def per_device(feat, nbr, mask, disp, radial, mixing, readout):
    vmem = pl.BlockSpec(memory_space=pltpu.VMEM)
    dma = pltpu.SemaphoreType.DMA
    tile = (8, 128)
    density = pl.pallas_call(
        kernel,
        out_shape=jax.ShapeDtypeStruct((1, PROBES), f32),
        in_specs=[pl.BlockSpec(memory_space=pl.ANY)] * 7,
        out_specs=vmem,
        scratch_shapes=[
            pltpu.VMEM((SLOTS, PROBES), jnp.int32),
            pltpu.VMEM((SLOTS, PROBES), jnp.int32),
            pltpu.VMEM((3, SLOTS, PROBES), f32),
            pltpu.VMEM((5, BASIS, CHAN), f32),
            pltpu.VMEM((128, 128), bf16),
            pltpu.VMEM((1, CHAN), f32),
            pltpu.VMEM((WINDOWS, ROWS, ATOMS), bf16),
            pltpu.VMEM((TABLE_ROWS, 128), f32),
            pltpu.VMEM((SLOTS, SLOT_ROWS, 128), f32),
            pltpu.VMEM((SLOT_ROWS, 128), f32),
            pltpu.VMEM((320, 128), f32),
            pltpu.VMEM((96, 1024), bf16),
            pltpu.VMEM((SLOTS, PROBES), jnp.int32),
            pltpu.VMEM((4, 128, 128), f32),
            pltpu.VMEM(tile, f32),
            pltpu.VMEM((PEERS,) + tile, f32),
            dma((6,)),
            dma((3, CHUNKS)),
            dma((WINDOWS, CHUNKS)),
            dma((CHUNKS,)),
            dma,
            dma((SLOTS,)),
            dma((5, PEERS)),
            dma((5, PEERS)),
        ]
        + [pltpu.SMEM((PROBES,), jnp.int32)] * SLOTS,
        compiler_params=pltpu.CompilerParams(
            collective_id=0, has_side_effects=True, vmem_limit_bytes=64 * 1024 * 1024 - 65536
        ),
    )(
        feat.reshape(ROWS, ATOMS),
        nbr,
        mask,
        disp,
        radial.transpose(1, 0, 2),
        mixing,
        readout.reshape(1, CHAN),
    )
    return density.reshape(PROBES)


def solution(mesh):
    return jax.shard_map(
        per_device,
        mesh=mesh,
        in_specs=(
            P(None, "ch", "dom"),
            P(None, "dom"),
            P(None, "dom"),
            P(None, None, "dom"),
            P(None, None, "ch"),
            P(),
            P("ch"),
        ),
        out_specs=P("dom"),
        check_vma=False,
    )
```
